32 devices in a mesh: dp: 8 (over z, y), tensor: 4 (over x, core).
Axes of the slice: x: 2, y: 2, z: 4, core: 2. Of those that a mesh axis runs over, the one named last changes fastest.
Arguments:
- tokens: bfloat16 [16384, 1024], P(('dp', 'tensor')), may hold values from -6 to 6
- out_grad: bfloat16 [16384, 1024], P(('dp', 'tensor')), may hold values from -6 to 6
- seq_lengths: int32 [8, 4], P('dp'), may hold values from 1 to 1536, as said below
- norm1_gain: float32 [1024], P(('dp', 'tensor')), may hold values from 0.5 to 1.5
- norm1_bias: float32 [1024], P(('dp', 'tensor')), may hold values from -1.25 to 1.25
- norm2_gain: float32 [1024], P(('dp', 'tensor')), may hold values from 0.5 to 1.5
- norm2_bias: float32 [1024], P(('dp', 'tensor')), may hold values from -1.25 to 1.25
- w_query: bfloat16 [1024, 1024], P('dp', 'tensor'), may hold values from -0.1875 to 0.1875
- b_query: float32 [1024], P(('dp', 'tensor')), may hold values from -1.25 to 1.25
- w_key: bfloat16 [1024, 1024], P('dp', 'tensor'), may hold values from -0.1875 to 0.1875
- b_key: float32 [1024], P(('dp', 'tensor')), may hold values from -1.25 to 1.25
- w_value: bfloat16 [1024, 1024], P('dp', 'tensor'), may hold values from -0.1875 to 0.1875
- b_value: float32 [1024], P(('dp', 'tensor')), may hold values from -1.25 to 1.25
- w_dense: bfloat16 [1024, 1024], P('tensor', 'dp'), may hold values from -3 to 3
- b_dense: float32 [1024], P(('dp', 'tensor')), may hold values from -1.25 to 1.25
- w_up: bfloat16 [1024, 4096], P('dp', 'tensor'), may hold values from -0.1875 to 0.1875
- b_up: float32 [4096], P(('dp', 'tensor')), may hold values from -1.25 to 1.25
- w_down: bfloat16 [4096, 1024], P('tensor', 'dp'), may hold values from -0.09375 to 0.09375
- b_down: float32 [1024], P(('dp', 'tensor')), may hold values from -1.25 to 1.25
Outputs:
- layer_out: bfloat16 [16384, 1024], P(('dp', 'tensor'))
- tokens_grad: float32 [16384, 1024], P(('dp', 'tensor'))
- grad_norm1_gain: float32 [1024], P(('dp', 'tensor'))
- grad_norm1_bias: float32 [1024], P(('dp', 'tensor'))
- grad_norm2_gain: float32 [1024], P(('dp', 'tensor'))
- grad_norm2_bias: float32 [1024], P(('dp', 'tensor'))
- grad_w_query: float32 [1024, 1024], P('dp', 'tensor')
- grad_b_query: float32 [1024], P(('dp', 'tensor'))
- grad_w_key: float32 [1024, 1024], P('dp', 'tensor')
- grad_b_key: float32 [1024], P(('dp', 'tensor'))
- grad_w_value: float32 [1024, 1024], P('dp', 'tensor')
- grad_b_value: float32 [1024], P(('dp', 'tensor'))
- grad_w_dense: float32 [1024, 1024], P('tensor', 'dp')
- grad_b_dense: float32 [1024], P(('dp', 'tensor'))
- grad_w_up: float32 [1024, 4096], P('dp', 'tensor')
- grad_b_up: float32 [4096], P(('dp', 'tensor'))
- grad_w_down: float32 [4096, 1024], P('tensor', 'dp')
- grad_b_down: float32 [1024], P(('dp', 'tensor'))
The draws below stay inside these ranges and needn't reach their ends.
Inputs may be any that keep to these rules, and one draw needn't show every extreme that they name: `seq_lengths`: each row gives the lengths of the 4 sequences packed in order into one group of 2048 tokens and sums to 2048. The second sequence of each row is exactly 1536 long and starts within the group's first 512 tokens; the other three together are 512 long.
All inputs are finite; a program needn't handle non-finite values.
Results may differ from the reference program's by a relative error of at most 0.01575.
Values may be sent and summed in bfloat16 or wider, within the bound.
A program may use at most 256 MiB of HBM per device.

```python
import math
import jax
import jax.numpy as jnp
from jax import lax

D = 1024
HEADS = 16
HEAD = 64
FF = 4096
ROTARY = 16
BLOCK = 512
GROUPS = 8
GROUP = 2048
LONGEST = 1536
TOKENS = 16384


def draw_seq_lengths(key, part):
    key = jax.random.fold_in(key, 7)
    first_key, split_key = jax.random.split(key)
    short_total = GROUP - LONGEST
    first_len = jax.random.randint(first_key, (GROUPS,), 1, short_total - 1)
    remaining = short_total - first_len
    cut_len = jax.random.randint(split_key, (GROUPS,), 1, remaining)
    long_len = jnp.full((GROUPS,), LONGEST, jnp.int32)
    return jnp.stack([first_len, long_len, cut_len, remaining - cut_len], axis=1).astype(jnp.int32)


def spiked(array, rng, source, target, blocks, factor):
    def block_of(position):
        return (jnp.arange(array.shape[position]) // (array.shape[position] // blocks)).reshape((-1,) + (1,) * (array.ndim - 1 - position))

    first = jax.random.permutation(rng, blocks)[block_of(target)]
    second = (block_of(target) + blocks // 2) % blocks
    return jnp.where((block_of(source) == first) | (block_of(source) == second), factor * array, array)


def levels(own_key, dims, pieces, low, high):
    level, own = 1.0, jax.random.fold_in(own_key, 6)
    for dim, shards_of in pieces:
        draws = jnp.exp(jax.random.uniform(jax.random.fold_in(own, dim), (shards_of,), jnp.float32, low / len(pieces), high / len(pieces)))
        level = level * jnp.repeat(draws, dims[dim] // shards_of).reshape([-1 if axis == dim else 1 for axis in range(len(dims))])
    return level


def noise(key, shape, width, reach, cuts=(), kind=jnp.bfloat16):
    result = width * jax.random.normal(key, shape, jnp.float32)
    if cuts:
        result = result * levels(key, shape, cuts, -0.22, 0.18)
    return jnp.clip(result, -reach, reach).astype(kind)


def heavy_noise(key, dims, deviation, reach, cuts, heavy, kind=jnp.bfloat16):
    entries = deviation * jax.random.normal(key, dims, jnp.float32)
    if cuts:
        entries = entries * levels(key, dims, cuts, -0.22, 0.18)
    return jnp.clip(spiked(entries, jax.random.fold_in(key, 3), *heavy), -reach, reach).astype(kind)


def setup_inputs(seed: int = 0) -> dict:
    key_of = jax.random.split(jax.random.key(seed), 20)
    tokens = noise(key_of[0], (TOKENS, D), 1.0, 6.0, ((0, 32),))
    out_grad = heavy_noise(key_of[1], (TOKENS, D), 1.0, 6.0, ((0, 32),), (0, 1, 32, 2.75))
    seq_lengths = draw_seq_lengths(jax.random.fold_in(key_of[19], 71), 0)
    norm1_gain = jnp.clip(1.0 + 0.1 * jax.random.normal(key_of[3], (D,), jnp.float32), 0.5, 1.5)
    norm1_bias = noise(key_of[4], (D,), 0.2, 1.25, ((0, 32),), jnp.float32)
    norm2_gain = jnp.clip(1.0 + 0.1 * jax.random.normal(key_of[5], (D,), jnp.float32), 0.5, 1.5)
    norm2_bias = noise(key_of[6], (D,), 0.2, 1.25, ((0, 32),), jnp.float32)
    w_query = noise(key_of[7], (D, D), D ** -0.5, 0.1875, ((0, 8), (1, 4)))
    b_query = noise(key_of[8], (D,), 0.2, 1.25, ((0, 32),), jnp.float32)
    w_key = noise(key_of[9], (D, D), D ** -0.5, 0.1875, ((0, 8), (1, 4)))
    b_key = noise(key_of[10], (D,), 0.2, 1.25, ((0, 32),), jnp.float32)
    w_value = noise(key_of[11], (D, D), D ** -0.5, 0.1875, ((0, 8), (1, 4)))
    b_value = noise(key_of[12], (D,), 0.2, 1.25, ((0, 32),), jnp.float32)
    w_dense = noise(key_of[13], (D, D), (HEAD // 16) ** -0.5, 3.0, ((0, 4), (1, 8)))
    b_dense = noise(key_of[14], (D,), 0.2, 1.25, ((0, 32),), jnp.float32)
    w_up = noise(key_of[15], (D, FF), D ** -0.5, 0.1875, ((0, 8), (1, 4)))
    b_up = noise(key_of[16], (FF,), 0.2, 1.25, ((0, 32),), jnp.float32)
    w_down = noise(key_of[17], (FF, D), FF ** -0.5, 0.09375, ((0, 4), (1, 8)))
    b_down = noise(key_of[18], (D,), 0.2, 1.25, ((0, 32),), jnp.float32)
    return dict(tokens=tokens, out_grad=out_grad, seq_lengths=seq_lengths, norm1_gain=norm1_gain, norm1_bias=norm1_bias, norm2_gain=norm2_gain, norm2_bias=norm2_bias, w_query=w_query, b_query=b_query, w_key=w_key, b_key=b_key, w_value=w_value, b_value=b_value, w_dense=w_dense, b_dense=b_dense, w_up=w_up, b_up=b_up, w_down=w_down, b_down=b_down)


EPS = 1e-05
MASKED_SCORE = -1e+30

@jax.custom_vjp
def low(v):
    return lax.optimization_barrier(v.astype(jnp.bfloat16)).astype(jnp.float32)

@jax.custom_vjp
def low_back(v):
    return v

def low_keep(v):
    return (low(v), None)

def low_pass(kept, grad):
    return (grad,)

def back_keep(v):
    return (v, None)

def back_low(kept, grad):
    return (low(grad),)
low.defvjp(low_keep, low_pass)
low_back.defvjp(back_keep, back_low)

def matmul_high(left, right):
    return jnp.dot(left, right, precision=lax.Precision.HIGHEST)

def layer_norm(row_vals, gain_vec, shift_vec):
    row_mean = lax.optimization_barrier(jnp.mean(row_vals, axis=-1, keepdims=True))
    centred = row_vals - row_mean
    row_var = lax.optimization_barrier(jnp.mean(centred * centred, axis=-1, keepdims=True))
    return centred * lax.rsqrt(row_var + EPS) * gain_vec + shift_vec

def smooth(values):
    return jax.nn.gelu(values, approximate=False)

def segment_rows(lengths, group_size):
    seq_ends = jnp.cumsum(lengths, dtype=jnp.int32)
    seq_starts = seq_ends - lengths
    row_index = jnp.arange(group_size, dtype=jnp.int32)
    segment = lax.optimization_barrier(jnp.sum((row_index[:, None] >= seq_ends[None, :]).astype(jnp.int32), axis=1, dtype=jnp.int32))
    seq_begin = lax.optimization_barrier(jnp.max(jnp.where(row_index[:, None] >= seq_starts[None, :], seq_starts[None, :], 0), axis=1))
    return (row_index, segment, (row_index - seq_begin).astype(jnp.float32))

def rotary_tables(positions, rot_dims):
    half_rot = rot_dims // 2
    frequency = 10000.0 ** (-2.0 * jnp.arange(half_rot, dtype=jnp.float32) / rot_dims)
    angles = positions[:, None] * frequency[None, :]
    cosine_half = jnp.cos(angles)
    sine_half = jnp.sin(angles)
    return (jnp.concatenate([cosine_half, cosine_half], 1), jnp.concatenate([sine_half, sine_half], 1))

def rotate(head_vals, cosine_table, sine_table):
    rot_dims = cosine_table.shape[1]
    half_rot = rot_dims // 2
    rot_part = head_vals[..., :rot_dims]
    turned = jnp.concatenate([-rot_part[..., half_rot:], rot_part[..., :half_rot]], -1)
    turned_part = rot_part * cosine_table[:, None, :] + turned * sine_table[:, None, :]
    return jnp.concatenate([turned_part, head_vals[..., rot_dims:]], -1)

def group_forward(rows_in, lengths, params):
    gain_one, shift_one, gain_two, shift_two, w_query, b_query, w_key, b_key, w_value, b_value, w_dense, b_dense, w_up, b_up, w_down, b_down = params
    group_size = rows_in.shape[0]
    row_index, segment, positions = segment_rows(lengths, group_size)
    cosine_table, sine_table = rotary_tables(positions, ROTARY)
    score_scale = 1.0 / math.sqrt(HEAD)
    normed_one = low(layer_norm(rows_in, gain_one, shift_one))
    normed_two = low(layer_norm(rows_in, gain_two, shift_two))
    query_pre = low_back(matmul_high(normed_one, w_query) + b_query)
    key_pre = low_back(matmul_high(normed_one, w_key) + b_key)
    queries = low(rotate(query_pre.reshape(group_size, HEADS, HEAD), cosine_table, sine_table))
    key_heads = low(rotate(key_pre.reshape(group_size, HEADS, HEAD), cosine_table, sine_table))
    values = low(low_back(matmul_high(normed_one, w_value) + b_value)).reshape(group_size, HEADS, HEAD)
    block_rows = min(BLOCK, group_size)

    def attend(block_in):
        query_blk, segment_blk, rows_blk = block_in
        scores = jnp.einsum('qhd,khd->hqk', query_blk, key_heads, precision=lax.Precision.HIGHEST) * score_scale
        scores = low_back(scores)
        allowed = (segment_blk[:, None] == segment[None, :]) & (rows_blk[:, None] >= row_index[None, :])
        scores = jnp.where(allowed[None], scores, MASKED_SCORE)
        attn_probs = low(jax.nn.softmax(scores, axis=-1))
        return jnp.einsum('hqk,khd->qhd', attn_probs, values, precision=lax.Precision.HIGHEST)
    blocks = group_size // block_rows
    context = lax.map(jax.checkpoint(attend), (queries.reshape(blocks, block_rows, HEADS, HEAD), segment.reshape(blocks, block_rows), row_index.reshape(blocks, block_rows)))
    context = low(low_back(context.reshape(group_size, D)))
    hidden = low_back(matmul_high(normed_two, w_up) + b_up)
    activated = low(smooth(hidden))
    return rows_in + matmul_high(context, w_dense) + matmul_high(activated, w_down) + b_dense + b_down

def reference(tokens, out_grad, seq_lengths, norm1_gain, norm1_bias, norm2_gain, norm2_bias, w_query, b_query, w_key, b_key, w_value, b_value, w_dense, b_dense, w_up, b_up, w_down, b_down):
    params = tuple((item.astype(jnp.float32) for item in (norm1_gain, norm1_bias, norm2_gain, norm2_bias, w_query, b_query, w_key, b_key, w_value, b_value, w_dense, b_dense, w_up, b_up, w_down, b_down)))
    group_count = seq_lengths.shape[0]
    rows_all = tokens.astype(jnp.float32).reshape(group_count, -1, D)

    def forward(rows_given, params_given):

        def one_group(carry, group_item):
            return (carry, group_forward(group_item[0], group_item[1], params_given))
        return lax.scan(one_group, jnp.zeros((), jnp.float32), (rows_given, seq_lengths))[1]
    outputs, pull_back = jax.vjp(forward, rows_all, params)
    rows_grad, param_grads = pull_back(out_grad.astype(jnp.float32).reshape(group_count, -1, D))
    layer_out = outputs.reshape(-1, D).astype(jnp.bfloat16)
    tokens_grad = rows_grad.reshape(-1, D)
    return (layer_out, tokens_grad, param_grads[0], param_grads[1], param_grads[2], param_grads[3], param_grads[4], param_grads[5], param_grads[6], param_grads[7], param_grads[8], param_grads[9], param_grads[10], param_grads[11], param_grads[12], param_grads[13], param_grads[14], param_grads[15])
```

```python
import functools
import math

import jax
import jax.numpy as jnp
from jax import lax
from jax.experimental import pallas as pl
from jax.experimental.pallas import tpu as pltpu
from jax.sharding import PartitionSpec as P

HEAD = 64
FF = 4096
ROTARY = 16
BLOCK = 512


EPS = 1e-05
MASKED_SCORE = -1e30


def layer_norm(row_vals, gain_vec, shift_vec):
    row_mean = jnp.mean(row_vals, axis=-1, keepdims=True)
    centred = row_vals - row_mean
    row_var = jnp.mean(centred * centred, axis=-1, keepdims=True)
    return centred * lax.rsqrt(row_var + EPS) * gain_vec + shift_vec


def smooth(values):
    return jax.nn.gelu(values, approximate=False)


def segment_rows(lengths, group_size):
    seq_ends = jnp.cumsum(lengths, dtype=jnp.int32)
    seq_starts = seq_ends - lengths
    row_index = jnp.arange(group_size, dtype=jnp.int32)
    segment = jnp.sum(
        (row_index[:, None] >= seq_ends[None, :]).astype(jnp.int32), axis=1, dtype=jnp.int32
    )
    seq_begin = jnp.max(
        jnp.where(row_index[:, None] >= seq_starts[None, :], seq_starts[None, :], 0), axis=1
    )
    return (row_index, segment, (row_index - seq_begin).astype(jnp.float32))


def rotary_tables(positions, rot_dims):
    half_rot = rot_dims // 2
    frequency = 10000.0 ** (-2.0 * jnp.arange(half_rot, dtype=jnp.float32) / rot_dims)
    angles = positions[:, None] * frequency[None, :]
    cosine_half = jnp.cos(angles)
    sine_half = jnp.sin(angles)
    return (
        jnp.concatenate([cosine_half, cosine_half], 1),
        jnp.concatenate([sine_half, sine_half], 1),
    )


def rotate(head_vals, cosine_table, sine_table):
    rot_dims = cosine_table.shape[1]
    half_rot = rot_dims // 2
    rot_part = head_vals[..., :rot_dims]
    turned = jnp.concatenate([-rot_part[..., half_rot:], rot_part[..., :half_rot]], -1)
    turned_part = rot_part * cosine_table[:, None, :] + turned * sine_table[:, None, :]
    return jnp.concatenate([turned_part, head_vals[..., rot_dims:]], -1)


RING = 8
VMEM_BYTES = 56 * 1024 * 1024
MESH_ID = pl.DeviceIdType.MESH
STREAMS = ((0, 0, 64, 1), (1, 0, 640, -1), (0, 64, 48, 1), (1, 640, 640, -1), (0, 112, 16, -1))


def ring_to_dp(place):
    place = (place + 2 * RING) % RING
    upper = place // (RING // 2)
    return 2 * place + upper * (2 * RING - 1 - 4 * place)


def partners():
    dp_at = lax.axis_index("dp")
    tensor_at = lax.axis_index("tensor")
    depth, side = dp_at // 2, dp_at % 2
    place = depth + side * (RING - 1 - 2 * depth)
    sibling = tensor_at + 1 - 2 * (tensor_at % 2)
    across = (tensor_at + 2) % 4
    return (dp_at, tensor_at, place, sibling, across)


def meet(devices):
    barrier = pltpu.get_barrier_semaphore()
    for device in devices:
        pl.semaphore_signal(barrier, inc=1, device_id=device, device_id_type=MESH_ID)
    pl.semaphore_wait(barrier, len(devices))


def remote(source, target, send, recv, device):
    return pltpu.make_async_remote_copy(
        src_ref=source,
        dst_ref=target,
        send_sem=send,
        recv_sem=recv,
        device_id=device,
        device_id_type=MESH_ID,
    )


def gather_kernel(
    tok, cot, small, w_in, w_out, tok_all, cot_all, small_all, in_all, out_all,
    local_sem, tsend, trecv, fsend, frecv, rsend, rrecv, ssend, srecv,
):
    dp_at, tensor_at, place, sibling, across = partners()
    right = (ring_to_dp(place + 1), tensor_at)
    left = (ring_to_dp(place - 1), tensor_at)
    sib = (dp_at, sibling)
    opp = (dp_at, across)
    meet((right, left, sib, opp))
    blocks = (w_in, w_out)
    fulls = (in_all, out_all)
    sends = []

    def ring_copy(number, step, owner):
        which, low, rows, way = STREAMS[number]
        here = fulls[which].at[owner, pl.ds(low, rows)]
        source = blocks[which].at[pl.ds(low, rows)] if step == 0 else here
        return remote(
            source, here, rsend.at[number, step], rrecv.at[number, step], right if way > 0 else left
        )

    def small_ring(step, owner):
        return remote(
            small_all.at[owner], small_all.at[owner], ssend.at[step], srecv.at[step], right
        )

    for number in range(len(STREAMS)):
        copy = ring_copy(number, 0, dp_at)
        copy.start()
        sends.append(copy)
    mine = ((small, small_all.at[dp_at]), (tok, tok_all), (cot, cot_all))
    for number, (own, full) in enumerate(mine):
        for peer, device in enumerate((opp, sib)):
            copy = remote(
                own, full.at[tensor_at], tsend.at[number, peer], trecv.at[number, peer], device
            )
            copy.start()
            sends.append(copy)
    locals_ = [
        pltpu.make_async_copy(own, full.at[tensor_at], local_sem.at[number])
        for number, (own, full) in enumerate(mine)
    ]
    locals_.append(pltpu.make_async_copy(w_in, in_all.at[dp_at], local_sem.at[3]))
    locals_.append(pltpu.make_async_copy(w_out, out_all.at[dp_at], local_sem.at[4]))
    for copy in locals_:
        copy.start()

    def forward(number):
        full = mine[number][1]
        remote(
            full.at[across], full.at[across], tsend.at[number, 0], trecv.at[number, 0], opp
        ).wait_recv()
        copy = remote(full.at[across], full.at[across], fsend.at[number], frecv.at[number], sib)
        copy.start()
        sends.append(copy)

    def settle(number):
        full = mine[number][1]
        remote(
            full.at[sibling], full.at[sibling], tsend.at[number, 1], trecv.at[number, 1], sib
        ).wait_recv()
        last = (sibling + 2) % 4
        remote(
            full.at[last], full.at[last], fsend.at[number], frecv.at[number], sib
        ).wait_recv()

    for copy in locals_:
        copy.wait()
    forward(0)
    settle(0)
    copy = small_ring(0, dp_at)
    copy.start()
    sends.append(copy)
    for step in range(1, RING):
        for number, (_, _, _, way) in enumerate(STREAMS):
            owner = ring_to_dp(place - way * step)
            arrived = fulls[STREAMS[number][0]].at[owner, pl.ds(STREAMS[number][1], STREAMS[number][2])]
            remote(
                arrived, arrived, rsend.at[number, step - 1], rrecv.at[number, step - 1], right
            ).wait_recv()
            if step < RING - 1:
                copy = ring_copy(number, step, owner)
                copy.start()
                sends.append(copy)
        owner = ring_to_dp(place - step)
        small_ring(step - 1, owner).wait_recv()
        if step < RING - 1:
            copy = small_ring(step, owner)
            copy.start()
            sends.append(copy)
        if step == 4:
            forward(1)
    forward(2)
    settle(1)
    settle(2)
    for copy in sends:
        copy.wait_send()


def gather_all(tok, cot, small, w_in, w_out):
    anywhere = pl.BlockSpec(memory_space=pl.ANY)
    shape = jax.ShapeDtypeStruct
    dma = pltpu.SemaphoreType.DMA
    return pl.pallas_call(
        gather_kernel,
        out_shape=(
            shape((4,) + tok.shape, tok.dtype),
            shape((4,) + cot.shape, cot.dtype),
            shape((RING, 4) + small.shape, small.dtype),
            shape((RING,) + w_in.shape, w_in.dtype),
            shape((RING,) + w_out.shape, w_out.dtype),
        ),
        in_specs=[anywhere] * 5,
        out_specs=(anywhere,) * 5,
        scratch_shapes=[
            dma((5,)),
            dma((3, 2)),
            dma((3, 2)),
            dma((3,)),
            dma((3,)),
            dma((len(STREAMS), RING - 1)),
            dma((len(STREAMS), RING - 1)),
            dma((RING - 1,)),
            dma((RING - 1,)),
        ],
        compiler_params=pltpu.CompilerParams(collective_id=0, has_side_effects=True),
    )(tok, cot, small, w_in, w_out)


def add_rows(target, terms, step):
    rows = target.shape[0]

    @pl.loop(0, rows // step)
    def _(at):
        here = pl.ds(pl.multiple_of(at * step, step), step)
        total = terms[0][here].astype(jnp.float32)
        for term in terms[1:]:
            total = total + term[here].astype(jnp.float32)
        target[here] = total.astype(target.dtype)


def scatter_kernel(
    parts, g_in, g_out, shares, own_in, own_out,
    slot_in, slot_out, core_buf, cross_buf, rsend, rrecv, csend, crecv, xsend, xrecv,
):
    dp_at, tensor_at, place, sibling, across = partners()
    right = (ring_to_dp(place + 1), tensor_at)
    left = (ring_to_dp(place - 1), tensor_at)
    sib = (dp_at, sibling)
    opp = (dp_at, across)
    meet((right, left, sib, opp))
    grads = (g_in, g_out)
    slots = (slot_in, slot_out)
    owns = (own_in, own_out)
    sends = []

    def slot_of(number, step):
        which, low, rows, _ = STREAMS[number]
        return slots[which].at[step, pl.ds(low, rows)]

    def grad_of(number, owner):
        which, low, rows, _ = STREAMS[number]
        return grads[which].at[owner, pl.ds(low, rows)]

    def ring_copy(number, step, source):
        way = STREAMS[number][3]
        return remote(
            source,
            slot_of(number, step),
            rsend.at[number, step],
            rrecv.at[number, step],
            right if way > 0 else left,
        )

    for number, (_, _, _, way) in enumerate(STREAMS):
        copy = ring_copy(number, 0, grad_of(number, ring_to_dp(place - way)))
        copy.start()
        sends.append(copy)
    count = parts.shape[0]
    across_sib = (sibling + 2) % 4
    for number in range(count):
        copy = remote(
            parts.at[number, across_sib],
            core_buf.at[number, 0],
            csend.at[number, 0],
            crecv.at[number, 0],
            sib,
        )
        copy.start()
        sends.append(copy)
    for number in range(count):
        copy = remote(
            parts.at[number, sibling],
            core_buf.at[number, 1],
            csend.at[number, 1],
            crecv.at[number, 1],
            sib,
        )
        copy.start()
        sends.append(copy)

    def cross(number):
        buf = core_buf.at[number, 0]
        remote(buf, buf, csend.at[number, 0], crecv.at[number, 0], sib).wait_recv()
        add_rows(buf, (buf, parts.at[number, across]), 64)
        copy = remote(buf, cross_buf.at[number], xsend.at[number], xrecv.at[number], opp)
        copy.start()
        sends.append(copy)

    for number in range(count):
        cross(number)
    for step in range(RING - 1):
        for number, (which, low, rows, way) in enumerate(STREAMS):
            here = slot_of(number, step)
            remote(
                here, here, rsend.at[number, step], rrecv.at[number, step], right
            ).wait_recv()
            term = grad_of(number, ring_to_dp(place - way * (2 + step)))
            if step < RING - 2:
                add_rows(here, (here, term), 80 if which else 16)
                copy = ring_copy(number, step + 1, here)
                copy.start()
                sends.append(copy)
            else:
                add_rows(owns[which].at[pl.ds(low, rows)], (here, term), 80 if which else 16)
    for number in range(count):
        buf = core_buf.at[number, 1]
        remote(buf, buf, csend.at[number, 1], crecv.at[number, 1], sib).wait_recv()
        other = cross_buf.at[number]
        remote(other, other, xsend.at[number], xrecv.at[number], opp).wait_recv()
        add_rows(shares.at[number], (buf, other, parts.at[number, tensor_at]), 64)
    for copy in sends:
        copy.wait_send()


def scatter_all(parts, g_in, g_out):
    inside = pl.BlockSpec(memory_space=pltpu.VMEM)
    shape = jax.ShapeDtypeStruct
    dma = pltpu.SemaphoreType.DMA
    count, _, rows, width = parts.shape
    return pl.pallas_call(
        scatter_kernel,
        out_shape=(
            shape((count, rows, width), jnp.bfloat16),
            shape(g_in.shape[1:], jnp.float32),
            shape(g_out.shape[1:], jnp.float32),
        ),
        in_specs=[inside] * 3,
        out_specs=(inside,) * 3,
        scratch_shapes=[
            pltpu.VMEM((RING - 1,) + g_in.shape[1:], jnp.bfloat16),
            pltpu.VMEM((RING - 1,) + g_out.shape[1:], jnp.bfloat16),
            pltpu.VMEM((count, 2, rows, width), jnp.bfloat16),
            pltpu.VMEM((count, rows, width), jnp.bfloat16),
            dma((len(STREAMS), RING - 1)),
            dma((len(STREAMS), RING - 1)),
            dma((count, 2)),
            dma((count, 2)),
            dma((count,)),
            dma((count,)),
        ],
        compiler_params=pltpu.CompilerParams(
            collective_id=1, has_side_effects=True, vmem_limit_bytes=VMEM_BYTES
        ),
    )(parts, g_in, g_out)


def sum_kernel(terms, total, first, middle, second, asend, arecv, bsend, brecv):
    dp_at = lax.axis_index("dp")
    tensor_at = lax.axis_index("tensor")
    peers = [(dp_at, (tensor_at + gap) % 4) for gap in range(1, 4)]
    rows = [((dp_at + gap) % RING, tensor_at) for gap in range(1, RING)]
    meet(peers + rows)
    sends = []
    for gap, device in enumerate(peers):
        copy = remote(
            terms.at[device[1]], first.at[gap], asend.at[gap], arecv.at[gap], device
        )
        copy.start()
        sends.append(copy)
    for copy in sends:
        copy.wait_recv()
    middle[...] = terms[tensor_at] + first[0] + first[1] + first[2]
    seconds = []
    for gap, device in enumerate(rows):
        copy = remote(
            middle.at[device[0]], second.at[gap], bsend.at[gap], brecv.at[gap], device
        )
        copy.start()
        seconds.append(copy)
    for copy in seconds:
        copy.wait_recv()
    result = middle[dp_at]
    for gap in range(RING - 1):
        result = result + second[gap]
    total[...] = result
    for copy in sends + seconds:
        copy.wait_send()


def sum_all(terms):
    inside = pl.BlockSpec(memory_space=pltpu.VMEM)
    dma = pltpu.SemaphoreType.DMA
    return pl.pallas_call(
        sum_kernel,
        out_shape=jax.ShapeDtypeStruct(terms.shape[2:], jnp.float32),
        in_specs=[inside],
        out_specs=inside,
        scratch_shapes=[
            pltpu.VMEM((3,) + terms.shape[1:], jnp.float32),
            pltpu.VMEM(terms.shape[1:], jnp.float32),
            pltpu.VMEM((RING - 1,) + terms.shape[2:], jnp.float32),
            dma((3,)),
            dma((3,)),
            dma((RING - 1,)),
            dma((RING - 1,)),
        ],
        compiler_params=pltpu.CompilerParams(collective_id=2, has_side_effects=True),
    )(terms)


def per_device(
    ring,
    tokens,
    out_grad,
    seq_lengths,
    norm1_gain,
    norm1_bias,
    norm2_gain,
    norm2_bias,
    w_query,
    b_query,
    w_key,
    b_key,
    w_value,
    b_value,
    w_dense,
    b_dense,
    w_up,
    b_up,
    w_down,
    b_down,
):
    vectors = (
        norm1_gain, norm1_bias, norm2_gain, norm2_bias,
        b_query, b_key, b_value, b_dense, b_down, b_up,
    )
    sizes = [vector.shape[0] for vector in vectors]
    packed = jnp.concatenate(vectors)
    w_in = jnp.concatenate([w_query, w_key, w_value, w_up], 1)
    w_out = jnp.concatenate([w_dense, w_down], 0)
    if ring:
        packed = jnp.pad(packed, (0, 1024 - packed.shape[0])).reshape(8, 128)
        tok_all, grad_group, packed_all, w_in, w_out = gather_all(
            tokens, out_grad, packed, w_in, w_out
        )
        tok_all = tok_all.reshape(-1, tokens.shape[1])
        grad_group = grad_group.reshape(-1, tokens.shape[1])
        packed_all = packed_all.reshape(4 * RING, 1024)
        w_in = w_in.reshape(-1, w_in.shape[2])
        w_out = w_out.transpose(1, 0, 2).reshape(w_out.shape[1], -1)
    else:
        packed_all = lax.all_gather(packed, ("dp", "tensor"), axis=0)
        packed_all = packed_all.reshape(-1, packed.shape[0])
        tok_all = lax.all_gather(tokens, "tensor", axis=0, tiled=True)
        grad_group = lax.all_gather(out_grad, "tensor", axis=0, tiled=True)
        w_in = lax.all_gather(w_in, "dp", axis=0, tiled=True)
        w_out = lax.all_gather(w_out, "dp", axis=1, tiled=True)
    gathered_small = []
    start = 0
    for size in sizes:
        gathered_small.append(packed_all[:, start : start + size].reshape(-1))
        start += size
    (
        gain_one,
        shift_one,
        gain_two,
        shift_two,
        bias_query,
        bias_key,
        bias_value,
        bias_dense,
        bias_down,
        bias_up,
    ) = gathered_small
    width = tokens.shape[1]
    column_count = w_query.shape[1]
    hidden_count = w_up.shape[1]
    heads_here = column_count // HEAD
    tensor_at = lax.axis_index("tensor")
    bias_query = lax.dynamic_slice_in_dim(bias_query, tensor_at * column_count, column_count)
    bias_key = lax.dynamic_slice_in_dim(bias_key, tensor_at * column_count, column_count)
    bias_value = lax.dynamic_slice_in_dim(bias_value, tensor_at * column_count, column_count)
    bias_up = lax.dynamic_slice_in_dim(bias_up, tensor_at * hidden_count, hidden_count)
    own_rows = tokens.astype(jnp.float32)
    all_rows = tok_all.astype(jnp.float32)
    normed_one = layer_norm(all_rows, gain_one, shift_one).astype(jnp.bfloat16)
    normed_two = layer_norm(all_rows, gain_two, shift_two).astype(jnp.bfloat16)
    group_size = normed_one.shape[0]
    row_index, segment, positions = segment_rows(seq_lengths.reshape(-1), group_size)
    cosine_table, sine_table = rotary_tables(positions, ROTARY)
    score_scale = 1.0 / math.sqrt(HEAD)
    w_qkv = w_in[:, : 3 * column_count]
    w_hidden = w_in[:, 3 * column_count :]
    qkv_raw = jnp.dot(normed_one, w_qkv, preferred_element_type=jnp.float32)
    query_raw = qkv_raw[:, :column_count]
    key_raw = qkv_raw[:, column_count : 2 * column_count]
    value_raw = qkv_raw[:, 2 * column_count :]
    up_raw = jnp.dot(normed_two, w_hidden, preferred_element_type=jnp.float32)
    queries = rotate(
        (query_raw + bias_query).reshape(group_size, heads_here, HEAD), cosine_table, sine_table
    ).astype(jnp.bfloat16)
    key_heads = rotate(
        (key_raw + bias_key).reshape(group_size, heads_here, HEAD), cosine_table, sine_table
    ).astype(jnp.bfloat16)
    values = (value_raw + bias_value).astype(jnp.bfloat16).reshape(group_size, heads_here, HEAD)
    block_rows = min(BLOCK, group_size)
    block_count = group_size // block_rows
    context_parts = []
    logsum_parts = []
    for block_at in range(block_count):
        low_row = block_at * block_rows
        high_row = low_row + block_rows
        allowed = (segment[low_row:high_row, None] == segment[None, :high_row]) & (
            row_index[low_row:high_row, None] >= row_index[None, :high_row]
        )
        scores = (
            jnp.einsum(
                "qhd,khd->hqk",
                queries[low_row:high_row],
                key_heads[:high_row],
                preferred_element_type=jnp.float32,
            )
            * score_scale
        )
        scores = jnp.where(allowed[None], scores, MASKED_SCORE)
        row_peak = jnp.max(scores, axis=-1, keepdims=True)
        expd = jnp.exp(scores - row_peak)
        row_total = jnp.sum(expd, axis=-1, keepdims=True)
        attn_probs = (expd / row_total).astype(jnp.bfloat16)
        context_parts.append(
            jnp.einsum(
                "hqk,khd->qhd", attn_probs, values[:high_row], preferred_element_type=jnp.float32
            )
        )
        logsum_parts.append(row_peak + jnp.log(row_total))
    context = (
        jnp.concatenate(context_parts, 0).reshape(group_size, column_count).astype(jnp.bfloat16)
    )
    hidden_pre = up_raw + bias_up
    activated = smooth(hidden_pre).astype(jnp.bfloat16)
    joined = jnp.concatenate([context, activated], 1)
    partial_cols = jnp.dot(joined, w_out, preferred_element_type=jnp.float32).astype(jnp.bfloat16)
    grad_out = jnp.einsum("gf,gd->fd", joined, grad_group, preferred_element_type=jnp.float32)
    grad_context = jnp.einsum(
        "gd,cd->gc", grad_group, w_out[:column_count], preferred_element_type=jnp.float32
    )
    grad_act = jnp.einsum(
        "gd,fd->gf", grad_group, w_out[column_count:], preferred_element_type=jnp.float32
    )
    grad_context = grad_context.astype(jnp.bfloat16).reshape(group_size, heads_here, HEAD)
    gelu_value, gelu_back = jax.vjp(smooth, hidden_pre)
    grad_hidden = gelu_back(grad_act)[0].astype(jnp.bfloat16)
    query_parts = []
    key_total = jnp.zeros((group_size, heads_here, HEAD), jnp.float32)
    value_total = jnp.zeros((group_size, heads_here, HEAD), jnp.float32)
    for block_at in range(block_count):
        low_row = block_at * block_rows
        high_row = low_row + block_rows
        allowed = (segment[low_row:high_row, None] == segment[None, :high_row]) & (
            row_index[low_row:high_row, None] >= row_index[None, :high_row]
        )
        query_blk = queries[low_row:high_row]
        scores = (
            jnp.einsum(
                "qhd,khd->hqk", query_blk, key_heads[:high_row], preferred_element_type=jnp.float32
            )
            * score_scale
        )
        scores = jnp.where(allowed[None], scores, MASKED_SCORE)
        probs_full = jnp.exp(scores - logsum_parts[block_at])
        grad_blk = grad_context[low_row:high_row]
        grad_probs = jnp.einsum(
            "qhd,khd->hqk", grad_blk, values[:high_row], preferred_element_type=jnp.float32
        )
        row_inner = jnp.sum(grad_probs * probs_full, axis=-1, keepdims=True)
        grad_scores = (probs_full * (grad_probs - row_inner)).astype(jnp.bfloat16)
        query_parts.append(
            jnp.einsum(
                "hqk,khd->qhd",
                grad_scores,
                key_heads[:high_row],
                preferred_element_type=jnp.float32,
            )
            * score_scale
        )
        key_total = key_total.at[:high_row].add(
            jnp.einsum("hqk,qhd->khd", grad_scores, query_blk, preferred_element_type=jnp.float32)
            * score_scale
        )
        value_total = value_total.at[:high_row].add(
            jnp.einsum(
                "hqk,qhd->khd",
                probs_full.astype(jnp.bfloat16),
                grad_blk,
                preferred_element_type=jnp.float32,
            )
        )
    rotated_zero, rotate_back = jax.vjp(
        lambda head_vals: rotate(head_vals, cosine_table, sine_table),
        jnp.zeros((group_size, heads_here, HEAD), jnp.float32),
    )
    grad_query = (
        rotate_back(jnp.concatenate(query_parts, 0))[0]
        .reshape(group_size, column_count)
        .astype(jnp.bfloat16)
    )
    grad_key = rotate_back(key_total)[0].reshape(group_size, column_count).astype(jnp.bfloat16)
    grad_value = value_total.reshape(group_size, column_count).astype(jnp.bfloat16)
    grad_qkv = jnp.concatenate([grad_query, grad_key, grad_value], 1)
    grad_wqkv = jnp.einsum("gd,gc->dc", normed_one, grad_qkv, preferred_element_type=jnp.float32)
    grad_wu = jnp.einsum("gd,gf->df", normed_two, grad_hidden, preferred_element_type=jnp.float32)
    part_one = jnp.einsum(
        "gc,dc->gd", grad_qkv, w_qkv, preferred_element_type=jnp.float32
    ).astype(jnp.bfloat16)
    part_two = jnp.einsum(
        "gf,df->gd", grad_hidden, w_hidden, preferred_element_type=jnp.float32
    ).astype(jnp.bfloat16)
    grad_in = jnp.concatenate(
        [grad_wqkv.astype(jnp.bfloat16), grad_wu.astype(jnp.bfloat16)], 1
    )
    grad_out = grad_out.astype(jnp.bfloat16)
    if ring:
        own_count = tokens.shape[0]
        parts = jnp.stack([partial_cols, part_one, part_two]).reshape(3, 4, own_count, width)
        shares, grad_in, grad_out = scatter_all(
            parts,
            grad_in.reshape(RING, width // RING, -1),
            grad_out.reshape(-1, RING, width // RING).transpose(1, 0, 2),
        )
        summed, share_one, share_two = (shares[number].astype(jnp.float32) for number in range(3))
    else:
        summed, share_one, share_two = (
            lax.psum_scatter(part, "tensor", scatter_dimension=0, tiled=True).astype(jnp.float32)
            for part in (partial_cols, part_one, part_two)
        )
        grad_in = lax.psum_scatter(grad_in, "dp", scatter_dimension=0, tiled=True)
        grad_out = lax.psum_scatter(grad_out, "dp", scatter_dimension=1, tiled=True)
    grad_in = grad_in.astype(jnp.float32)
    grad_out = grad_out.astype(jnp.float32)
    grads_in = (
        grad_in[:, :column_count],
        grad_in[:, column_count : 2 * column_count],
        grad_in[:, 2 * column_count : 3 * column_count],
        grad_in[:, 3 * column_count :],
    )
    grad_dense, grad_down = grad_out[:column_count], grad_out[column_count:]
    layer_out = (own_rows + summed + bias_dense + bias_down).astype(jnp.bfloat16)
    normed_val_one, back_one = jax.vjp(layer_norm, own_rows, gain_one, shift_one)
    normed_val_two, back_two = jax.vjp(layer_norm, own_rows, gain_two, shift_two)
    input_one, d_gain_one, d_shift_one = back_one(share_one)
    input_two, d_gain_two, d_shift_two = back_two(share_two)
    tokens_grad = out_grad.astype(jnp.float32) + input_one + input_two

    def placed(vector, full_len):
        return lax.dynamic_update_slice_in_dim(
            jnp.zeros((full_len,), jnp.float32), vector, tensor_at * vector.shape[0], 0
        )

    bias_sum = jnp.sum(out_grad, axis=0, dtype=jnp.float32)
    devices = packed_all.shape[0]
    small_terms = jnp.concatenate(
        [
            vector.reshape(devices, -1)
            for vector in (
                d_gain_one,
                d_shift_one,
                d_gain_two,
                d_shift_two,
                placed(jnp.sum(grad_query, axis=0, dtype=jnp.float32), width),
                placed(jnp.sum(grad_key, axis=0, dtype=jnp.float32), width),
                placed(jnp.sum(grad_value, axis=0, dtype=jnp.float32), width),
                bias_sum,
                placed(jnp.sum(grad_hidden, axis=0, dtype=jnp.float32), FF),
            )
        ],
        1,
    )
    if ring:
        small_terms = jnp.pad(small_terms, ((0, 0), (0, 1024 - small_terms.shape[1])))
        small_terms = small_terms.reshape(RING, 4, 8, 128).transpose(1, 0, 2, 3)
        small_total = sum_all(small_terms).reshape(-1)
    else:
        small_total = lax.psum_scatter(
            small_terms, ("dp", "tensor"), scatter_dimension=0, tiled=True
        ).reshape(-1)
    each = width // devices
    small_grads = [small_total[at * each : (at + 1) * each] for at in range(8)]
    small_grads.append(small_total[8 * each : 8 * each + FF // devices])
    return (
        layer_out,
        tokens_grad,
        small_grads[0],
        small_grads[1],
        small_grads[2],
        small_grads[3],
        grads_in[0],
        small_grads[4],
        grads_in[1],
        small_grads[5],
        grads_in[2],
        small_grads[6],
        grad_dense,
        small_grads[7],
        grads_in[3],
        small_grads[8],
        grad_down,
        small_grads[7],
    )


def solution(mesh):
    in_specs = (
        P(("dp", "tensor"), None),
        P(("dp", "tensor"), None),
        P("dp", None),
        P(("dp", "tensor")),
        P(("dp", "tensor")),
        P(("dp", "tensor")),
        P(("dp", "tensor")),
        P("dp", "tensor"),
        P(("dp", "tensor")),
        P("dp", "tensor"),
        P(("dp", "tensor")),
        P("dp", "tensor"),
        P(("dp", "tensor")),
        P("tensor", "dp"),
        P(("dp", "tensor")),
        P("dp", "tensor"),
        P(("dp", "tensor")),
        P("tensor", "dp"),
        P(("dp", "tensor")),
    )
    out_specs = (
        P(("dp", "tensor"), None),
        P(("dp", "tensor"), None),
        P(("dp", "tensor")),
        P(("dp", "tensor")),
        P(("dp", "tensor")),
        P(("dp", "tensor")),
        P("dp", "tensor"),
        P(("dp", "tensor")),
        P("dp", "tensor"),
        P(("dp", "tensor")),
        P("dp", "tensor"),
        P(("dp", "tensor")),
        P("tensor", "dp"),
        P(("dp", "tensor")),
        P("dp", "tensor"),
        P(("dp", "tensor")),
        P("tensor", "dp"),
        P(("dp", "tensor")),
    )
    ring = mesh.shape["dp"] == RING and mesh.shape["tensor"] == 4
    return jax.shard_map(
        functools.partial(per_device, ring), mesh=mesh, in_specs=in_specs, out_specs=out_specs, check_vma=False
    )
```

```python
import functools
import math

import jax
import jax.numpy as jnp
from jax import lax
from jax.experimental import pallas as pl
from jax.experimental.pallas import tpu as pltpu
from jax.sharding import PartitionSpec as P

HEAD = 64
FF = 4096
ROTARY = 16
BLOCK = 512


EPS = 1e-05
MASKED_SCORE = -1e30


def layer_norm(row_vals, gain_vec, shift_vec):
    row_mean = jnp.mean(row_vals, axis=-1, keepdims=True)
    centred = row_vals - row_mean
    row_var = jnp.mean(centred * centred, axis=-1, keepdims=True)
    return centred * lax.rsqrt(row_var + EPS) * gain_vec + shift_vec


def smooth_and_slope(values):
    below = 0.5 * (1.0 + lax.erf(values * math.sqrt(0.5)))
    density = jnp.exp(-0.5 * values * values) * (1.0 / math.sqrt(2.0 * math.pi))
    return (values * below, below + values * density)


def segment_rows(lengths, group_size):
    seq_ends = jnp.cumsum(lengths, dtype=jnp.int32)
    seq_starts = seq_ends - lengths
    row_index = jnp.arange(group_size, dtype=jnp.int32)
    segment = jnp.sum(
        (row_index[:, None] >= seq_ends[None, :]).astype(jnp.int32), axis=1, dtype=jnp.int32
    )
    seq_begin = jnp.max(
        jnp.where(row_index[:, None] >= seq_starts[None, :], seq_starts[None, :], 0), axis=1
    )
    return (row_index, segment, (row_index - seq_begin).astype(jnp.float32))


def rotary_tables(positions, rot_dims):
    half_rot = rot_dims // 2
    frequency = 10000.0 ** (-2.0 * jnp.arange(half_rot, dtype=jnp.float32) / rot_dims)
    angles = positions[:, None] * frequency[None, :]
    cosine_half = jnp.cos(angles)
    sine_half = jnp.sin(angles)
    return (
        jnp.concatenate([cosine_half, cosine_half], 1),
        jnp.concatenate([sine_half, sine_half], 1),
    )


def rotate(head_vals, cosine_table, sine_table):
    rot_dims = cosine_table.shape[1]
    half_rot = rot_dims // 2
    rot_part = head_vals[..., :rot_dims]
    turned = jnp.concatenate([-rot_part[..., half_rot:], rot_part[..., :half_rot]], -1)
    turned_part = rot_part * cosine_table[:, None, :] + turned * sine_table[:, None, :]
    return jnp.concatenate([turned_part, head_vals[..., rot_dims:]], -1)


RING = 8
VMEM_BYTES = 56 * 1024 * 1024
MESH_ID = pl.DeviceIdType.MESH
STREAMS = ((0, 0, 64, 1), (1, 0, 640, -1), (0, 64, 48, 1), (1, 640, 640, -1), (0, 112, 16, -1))


def ring_to_dp(place):
    place = (place + 2 * RING) % RING
    upper = place // (RING // 2)
    return 2 * place + upper * (2 * RING - 1 - 4 * place)


def partners():
    dp_at = lax.axis_index("dp")
    tensor_at = lax.axis_index("tensor")
    depth, side = dp_at // 2, dp_at % 2
    place = depth + side * (RING - 1 - 2 * depth)
    sibling = tensor_at + 1 - 2 * (tensor_at % 2)
    across = (tensor_at + 2) % 4
    return (dp_at, tensor_at, place, sibling, across)


def meet(devices):
    barrier = pltpu.get_barrier_semaphore()
    for device in devices:
        pl.semaphore_signal(barrier, inc=1, device_id=device, device_id_type=MESH_ID)
    pl.semaphore_wait(barrier, len(devices))


def remote(source, target, send, recv, device):
    return pltpu.make_async_remote_copy(
        src_ref=source,
        dst_ref=target,
        send_sem=send,
        recv_sem=recv,
        device_id=device,
        device_id_type=MESH_ID,
    )


def gather_kernel(
    tok, cot, small, w_in, w_out, tok_all, cot_all, small_all, in_all, out_all,
    local_sem, tsend, trecv, fsend, frecv, rsend, rrecv, ssend, srecv,
):
    dp_at, tensor_at, place, sibling, across = partners()
    right = (ring_to_dp(place + 1), tensor_at)
    left = (ring_to_dp(place - 1), tensor_at)
    sib = (dp_at, sibling)
    opp = (dp_at, across)
    meet((right, left, sib, opp))
    blocks = (w_in, w_out)
    fulls = (in_all, out_all)
    sends = []

    def ring_copy(number, step, owner):
        which, low, rows, way = STREAMS[number]
        here = fulls[which].at[owner, pl.ds(low, rows)]
        source = blocks[which].at[pl.ds(low, rows)] if step == 0 else here
        return remote(
            source, here, rsend.at[number, step], rrecv.at[number, step], right if way > 0 else left
        )

    def small_ring(step, owner):
        return remote(
            small_all.at[owner], small_all.at[owner], ssend.at[step], srecv.at[step], right
        )

    for number in range(len(STREAMS)):
        copy = ring_copy(number, 0, dp_at)
        copy.start()
        sends.append(copy)
    mine = ((small, small_all.at[dp_at]), (tok, tok_all), (cot, cot_all))
    for number, (own, full) in enumerate(mine):
        for peer, device in enumerate((opp, sib)):
            copy = remote(
                own, full.at[tensor_at], tsend.at[number, peer], trecv.at[number, peer], device
            )
            copy.start()
            sends.append(copy)
    locals_ = [
        pltpu.make_async_copy(own, full.at[tensor_at], local_sem.at[number])
        for number, (own, full) in enumerate(mine)
    ]
    locals_.append(pltpu.make_async_copy(w_in, in_all.at[dp_at], local_sem.at[3]))
    locals_.append(pltpu.make_async_copy(w_out, out_all.at[dp_at], local_sem.at[4]))
    for copy in locals_:
        copy.start()

    def forward(number):
        full = mine[number][1]
        remote(
            full.at[across], full.at[across], tsend.at[number, 0], trecv.at[number, 0], opp
        ).wait_recv()
        copy = remote(full.at[across], full.at[across], fsend.at[number], frecv.at[number], sib)
        copy.start()
        sends.append(copy)

    def settle(number):
        full = mine[number][1]
        remote(
            full.at[sibling], full.at[sibling], tsend.at[number, 1], trecv.at[number, 1], sib
        ).wait_recv()
        last = (sibling + 2) % 4
        remote(
            full.at[last], full.at[last], fsend.at[number], frecv.at[number], sib
        ).wait_recv()

    for copy in locals_:
        copy.wait()
    forward(0)
    settle(0)
    copy = small_ring(0, dp_at)
    copy.start()
    sends.append(copy)
    for step in range(1, RING):
        for number, (_, _, _, way) in enumerate(STREAMS):
            owner = ring_to_dp(place - way * step)
            arrived = fulls[STREAMS[number][0]].at[owner, pl.ds(STREAMS[number][1], STREAMS[number][2])]
            remote(
                arrived, arrived, rsend.at[number, step - 1], rrecv.at[number, step - 1], right
            ).wait_recv()
            if step < RING - 1:
                copy = ring_copy(number, step, owner)
                copy.start()
                sends.append(copy)
        owner = ring_to_dp(place - step)
        small_ring(step - 1, owner).wait_recv()
        if step < RING - 1:
            copy = small_ring(step, owner)
            copy.start()
            sends.append(copy)
        if step == 4:
            forward(1)
    forward(2)
    settle(1)
    settle(2)
    for copy in sends:
        copy.wait_send()


def gather_all(tok, cot, small, w_in, w_out):
    inside = pl.BlockSpec(memory_space=pltpu.VMEM)
    shape = jax.ShapeDtypeStruct
    dma = pltpu.SemaphoreType.DMA
    return pl.pallas_call(
        gather_kernel,
        out_shape=(
            shape((4,) + tok.shape, tok.dtype),
            shape((4,) + cot.shape, cot.dtype),
            shape((RING, 4) + small.shape, small.dtype),
            shape((RING,) + w_in.shape, w_in.dtype),
            shape((RING,) + w_out.shape, w_out.dtype),
        ),
        in_specs=[inside] * 5,
        out_specs=(inside,) * 5,
        scratch_shapes=[
            dma((5,)),
            dma((3, 2)),
            dma((3, 2)),
            dma((3,)),
            dma((3,)),
            dma((len(STREAMS), RING - 1)),
            dma((len(STREAMS), RING - 1)),
            dma((RING - 1,)),
            dma((RING - 1,)),
        ],
        compiler_params=pltpu.CompilerParams(
            collective_id=0, has_side_effects=True, vmem_limit_bytes=VMEM_BYTES
        ),
    )(tok, cot, small, w_in, w_out)


def add_rows(target, terms, step):
    rows = target.shape[0]

    @pl.loop(0, rows // step)
    def _(at):
        here = pl.ds(pl.multiple_of(at * step, step), step)
        total = terms[0][here].astype(jnp.float32)
        for term in terms[1:]:
            total = total + term[here].astype(jnp.float32)
        target[here] = total.astype(target.dtype)


def scatter_kernel(
    parts, g_in, g_out, shares, own_in, own_out,
    slot_in, slot_out, core_buf, cross_buf, rsend, rrecv, csend, crecv, xsend, xrecv,
):
    dp_at, tensor_at, place, sibling, across = partners()
    right = (ring_to_dp(place + 1), tensor_at)
    left = (ring_to_dp(place - 1), tensor_at)
    sib = (dp_at, sibling)
    opp = (dp_at, across)
    meet((right, left, sib, opp))
    grads = (g_in, g_out)
    slots = (slot_in, slot_out)
    owns = (own_in, own_out)
    sends = []

    def slot_of(number, step):
        which, low, rows, _ = STREAMS[number]
        return slots[which].at[step, pl.ds(low, rows)]

    def grad_of(number, owner):
        which, low, rows, _ = STREAMS[number]
        return grads[which].at[owner, pl.ds(low, rows)]

    def ring_copy(number, step, source):
        way = STREAMS[number][3]
        return remote(
            source,
            slot_of(number, step),
            rsend.at[number, step],
            rrecv.at[number, step],
            right if way > 0 else left,
        )

    for number, (_, _, _, way) in enumerate(STREAMS):
        copy = ring_copy(number, 0, grad_of(number, ring_to_dp(place - way)))
        copy.start()
        sends.append(copy)
    count = parts.shape[0]
    across_sib = (sibling + 2) % 4
    for number in range(count):
        copy = remote(
            parts.at[number, across_sib],
            core_buf.at[number, 0],
            csend.at[number, 0],
            crecv.at[number, 0],
            sib,
        )
        copy.start()
        sends.append(copy)
    for number in range(count):
        copy = remote(
            parts.at[number, sibling],
            core_buf.at[number, 1],
            csend.at[number, 1],
            crecv.at[number, 1],
            sib,
        )
        copy.start()
        sends.append(copy)

    def cross(number):
        buf = core_buf.at[number, 0]
        remote(buf, buf, csend.at[number, 0], crecv.at[number, 0], sib).wait_recv()
        add_rows(buf, (buf, parts.at[number, across]), 64)
        copy = remote(buf, cross_buf.at[number], xsend.at[number], xrecv.at[number], opp)
        copy.start()
        sends.append(copy)

    for number in range(count):
        cross(number)
    for step in range(RING - 1):
        for number, (which, low, rows, way) in enumerate(STREAMS):
            here = slot_of(number, step)
            remote(
                here, here, rsend.at[number, step], rrecv.at[number, step], right
            ).wait_recv()
            term = grad_of(number, ring_to_dp(place - way * (2 + step)))
            if step < RING - 2:
                add_rows(here, (here, term), 80 if which else 16)
                copy = ring_copy(number, step + 1, here)
                copy.start()
                sends.append(copy)
            else:
                add_rows(owns[which].at[pl.ds(low, rows)], (here, term), 80 if which else 16)
    for number in range(count):
        buf = core_buf.at[number, 1]
        remote(buf, buf, csend.at[number, 1], crecv.at[number, 1], sib).wait_recv()
        other = cross_buf.at[number]
        remote(other, other, xsend.at[number], xrecv.at[number], opp).wait_recv()
        add_rows(shares.at[number], (buf, other, parts.at[number, tensor_at]), 64)
    for copy in sends:
        copy.wait_send()


def scatter_all(parts, g_in, g_out):
    inside = pl.BlockSpec(memory_space=pltpu.VMEM)
    shape = jax.ShapeDtypeStruct
    dma = pltpu.SemaphoreType.DMA
    count, _, rows, width = parts.shape
    return pl.pallas_call(
        scatter_kernel,
        out_shape=(
            shape((count, rows, width), jnp.bfloat16),
            shape(g_in.shape[1:], jnp.float32),
            shape(g_out.shape[1:], jnp.float32),
        ),
        in_specs=[inside] * 3,
        out_specs=(inside,) * 3,
        scratch_shapes=[
            pltpu.VMEM((RING - 1,) + g_in.shape[1:], jnp.bfloat16),
            pltpu.VMEM((RING - 1,) + g_out.shape[1:], jnp.bfloat16),
            pltpu.VMEM((count, 2, rows, width), jnp.bfloat16),
            pltpu.VMEM((count, rows, width), jnp.bfloat16),
            dma((len(STREAMS), RING - 1)),
            dma((len(STREAMS), RING - 1)),
            dma((count, 2)),
            dma((count, 2)),
            dma((count,)),
            dma((count,)),
        ],
        compiler_params=pltpu.CompilerParams(
            collective_id=1, has_side_effects=True, vmem_limit_bytes=VMEM_BYTES
        ),
    )(parts, g_in, g_out)


def sum_kernel(terms, total, first, middle, second, asend, arecv, bsend, brecv):
    dp_at = lax.axis_index("dp")
    tensor_at = lax.axis_index("tensor")
    peers = [(dp_at, (tensor_at + gap) % 4) for gap in range(1, 4)]
    rows = [((dp_at + gap) % RING, tensor_at) for gap in range(1, RING)]
    meet(peers + rows)
    sends = []
    for gap, device in enumerate(peers):
        copy = remote(
            terms.at[device[1]], first.at[gap], asend.at[gap], arecv.at[gap], device
        )
        copy.start()
        sends.append(copy)
    for copy in sends:
        copy.wait_recv()
    middle[...] = terms[tensor_at] + first[0] + first[1] + first[2]
    seconds = []
    for gap, device in enumerate(rows):
        copy = remote(
            middle.at[device[0]], second.at[gap], bsend.at[gap], brecv.at[gap], device
        )
        copy.start()
        seconds.append(copy)
    for copy in seconds:
        copy.wait_recv()
    result = middle[dp_at]
    for gap in range(RING - 1):
        result = result + second[gap]
    total[...] = result
    for copy in sends + seconds:
        copy.wait_send()


def sum_all(terms):
    inside = pl.BlockSpec(memory_space=pltpu.VMEM)
    dma = pltpu.SemaphoreType.DMA
    return pl.pallas_call(
        sum_kernel,
        out_shape=jax.ShapeDtypeStruct(terms.shape[2:], jnp.float32),
        in_specs=[inside],
        out_specs=inside,
        scratch_shapes=[
            pltpu.VMEM((3,) + terms.shape[1:], jnp.float32),
            pltpu.VMEM(terms.shape[1:], jnp.float32),
            pltpu.VMEM((RING - 1,) + terms.shape[2:], jnp.float32),
            dma((3,)),
            dma((3,)),
            dma((RING - 1,)),
            dma((RING - 1,)),
        ],
        compiler_params=pltpu.CompilerParams(collective_id=2, has_side_effects=True),
    )(terms)


def per_device(
    ring,
    tokens,
    out_grad,
    seq_lengths,
    norm1_gain,
    norm1_bias,
    norm2_gain,
    norm2_bias,
    w_query,
    b_query,
    w_key,
    b_key,
    w_value,
    b_value,
    w_dense,
    b_dense,
    w_up,
    b_up,
    w_down,
    b_down,
):
    vectors = (
        norm1_gain, norm1_bias, norm2_gain, norm2_bias,
        b_query, b_key, b_value, b_dense, b_down, b_up,
    )
    sizes = [vector.shape[0] for vector in vectors]
    packed = jnp.concatenate(vectors)
    w_in = jnp.concatenate([w_query, w_key, w_value, w_up], 1)
    w_out = jnp.concatenate([w_dense, w_down], 0)
    if ring:
        packed = jnp.pad(packed, (0, 1024 - packed.shape[0])).reshape(8, 128)
        tok_all, grad_group, packed_all, w_in, w_out = gather_all(
            tokens, out_grad, packed, w_in, w_out
        )
        tok_all = tok_all.reshape(-1, tokens.shape[1])
        grad_group = grad_group.reshape(-1, tokens.shape[1])
        packed_all = packed_all.reshape(4 * RING, 1024)
        w_in = w_in.reshape(-1, w_in.shape[2])
        w_out = w_out.transpose(1, 0, 2).reshape(w_out.shape[1], -1)
    else:
        packed_all = lax.all_gather(packed, ("dp", "tensor"), axis=0)
        packed_all = packed_all.reshape(-1, packed.shape[0])
        tok_all = lax.all_gather(tokens, "tensor", axis=0, tiled=True)
        grad_group = lax.all_gather(out_grad, "tensor", axis=0, tiled=True)
        w_in = lax.all_gather(w_in, "dp", axis=0, tiled=True)
        w_out = lax.all_gather(w_out, "dp", axis=1, tiled=True)
    gathered_small = []
    start = 0
    for size in sizes:
        gathered_small.append(packed_all[:, start : start + size].reshape(-1))
        start += size
    (
        gain_one,
        shift_one,
        gain_two,
        shift_two,
        bias_query,
        bias_key,
        bias_value,
        bias_dense,
        bias_down,
        bias_up,
    ) = gathered_small
    width = tokens.shape[1]
    column_count = w_query.shape[1]
    hidden_count = w_up.shape[1]
    heads_here = column_count // HEAD
    tensor_at = lax.axis_index("tensor")
    bias_query = lax.dynamic_slice_in_dim(bias_query, tensor_at * column_count, column_count)
    bias_key = lax.dynamic_slice_in_dim(bias_key, tensor_at * column_count, column_count)
    bias_value = lax.dynamic_slice_in_dim(bias_value, tensor_at * column_count, column_count)
    bias_up = lax.dynamic_slice_in_dim(bias_up, tensor_at * hidden_count, hidden_count)
    own_rows = tokens.astype(jnp.float32)
    all_rows = tok_all.astype(jnp.float32)
    normed_one = layer_norm(all_rows, gain_one, shift_one).astype(jnp.bfloat16)
    normed_two = layer_norm(all_rows, gain_two, shift_two).astype(jnp.bfloat16)
    group_size = normed_one.shape[0]
    row_index, segment, positions = segment_rows(seq_lengths.reshape(-1), group_size)
    cosine_table, sine_table = rotary_tables(positions, ROTARY)
    score_scale = 1.0 / math.sqrt(HEAD)
    w_qkv = w_in[:, : 3 * column_count]
    w_hidden = w_in[:, 3 * column_count :]
    qkv_raw = jnp.dot(normed_one, w_qkv, preferred_element_type=jnp.float32)
    query_raw = qkv_raw[:, :column_count]
    key_raw = qkv_raw[:, column_count : 2 * column_count]
    value_raw = qkv_raw[:, 2 * column_count :]
    up_raw = jnp.dot(normed_two, w_hidden, preferred_element_type=jnp.float32)
    queries = rotate(
        (query_raw + bias_query).reshape(group_size, heads_here, HEAD), cosine_table, sine_table
    ).astype(jnp.bfloat16)
    key_heads = rotate(
        (key_raw + bias_key).reshape(group_size, heads_here, HEAD), cosine_table, sine_table
    ).astype(jnp.bfloat16)
    values = (value_raw + bias_value).astype(jnp.bfloat16).reshape(group_size, heads_here, HEAD)
    block_rows = min(BLOCK, group_size)
    block_count = group_size // block_rows
    context_parts = []
    logsum_parts = []
    for block_at in range(block_count):
        low_row = block_at * block_rows
        high_row = low_row + block_rows
        allowed = (segment[low_row:high_row, None] == segment[None, :high_row]) & (
            row_index[low_row:high_row, None] >= row_index[None, :high_row]
        )
        scores = (
            jnp.einsum(
                "qhd,khd->hqk",
                queries[low_row:high_row],
                key_heads[:high_row],
                preferred_element_type=jnp.float32,
            )
            * score_scale
        )
        scores = jnp.where(allowed[None], scores, MASKED_SCORE)
        row_peak = jnp.max(scores, axis=-1, keepdims=True)
        expd = jnp.exp(scores - row_peak)
        row_total = jnp.sum(expd, axis=-1, keepdims=True)
        attn_probs = (expd / row_total).astype(jnp.bfloat16)
        context_parts.append(
            jnp.einsum(
                "hqk,khd->qhd", attn_probs, values[:high_row], preferred_element_type=jnp.float32
            )
        )
        logsum_parts.append(row_peak + jnp.log(row_total))
    context = (
        jnp.concatenate(context_parts, 0).reshape(group_size, column_count).astype(jnp.bfloat16)
    )
    hidden_pre = up_raw + bias_up
    activated, slope = smooth_and_slope(hidden_pre)
    activated, slope = lax.optimization_barrier((activated.astype(jnp.bfloat16), slope))
    joined = jnp.concatenate([context, activated], 1)
    partial_cols = jnp.dot(joined, w_out, preferred_element_type=jnp.float32).astype(jnp.bfloat16)
    grad_out = jnp.einsum("gf,gd->fd", joined, grad_group, preferred_element_type=jnp.float32)
    grad_context = jnp.einsum(
        "gd,cd->gc", grad_group, w_out[:column_count], preferred_element_type=jnp.float32
    )
    grad_act = jnp.einsum(
        "gd,fd->gf", grad_group, w_out[column_count:], preferred_element_type=jnp.float32
    )
    grad_context = grad_context.astype(jnp.bfloat16).reshape(group_size, heads_here, HEAD)
    grad_hidden = (grad_act * slope).astype(jnp.bfloat16)
    query_parts = []
    key_total = jnp.zeros((group_size, heads_here, HEAD), jnp.float32)
    value_total = jnp.zeros((group_size, heads_here, HEAD), jnp.float32)
    for block_at in range(block_count):
        low_row = block_at * block_rows
        high_row = low_row + block_rows
        allowed = (segment[low_row:high_row, None] == segment[None, :high_row]) & (
            row_index[low_row:high_row, None] >= row_index[None, :high_row]
        )
        query_blk = queries[low_row:high_row]
        scores = (
            jnp.einsum(
                "qhd,khd->hqk", query_blk, key_heads[:high_row], preferred_element_type=jnp.float32
            )
            * score_scale
        )
        scores = jnp.where(allowed[None], scores, MASKED_SCORE)
        probs_full = jnp.exp(scores - logsum_parts[block_at])
        grad_blk = grad_context[low_row:high_row]
        grad_probs = jnp.einsum(
            "qhd,khd->hqk", grad_blk, values[:high_row], preferred_element_type=jnp.float32
        )
        row_inner = jnp.sum(grad_probs * probs_full, axis=-1, keepdims=True)
        grad_scores = (probs_full * (grad_probs - row_inner)).astype(jnp.bfloat16)
        query_parts.append(
            jnp.einsum(
                "hqk,khd->qhd",
                grad_scores,
                key_heads[:high_row],
                preferred_element_type=jnp.float32,
            )
            * score_scale
        )
        key_total = key_total.at[:high_row].add(
            jnp.einsum("hqk,qhd->khd", grad_scores, query_blk, preferred_element_type=jnp.float32)
            * score_scale
        )
        value_total = value_total.at[:high_row].add(
            jnp.einsum(
                "hqk,qhd->khd",
                probs_full.astype(jnp.bfloat16),
                grad_blk,
                preferred_element_type=jnp.float32,
            )
        )
    rotated_zero, rotate_back = jax.vjp(
        lambda head_vals: rotate(head_vals, cosine_table, sine_table),
        jnp.zeros((group_size, heads_here, HEAD), jnp.float32),
    )
    grad_query = (
        rotate_back(jnp.concatenate(query_parts, 0))[0]
        .reshape(group_size, column_count)
        .astype(jnp.bfloat16)
    )
    grad_key = rotate_back(key_total)[0].reshape(group_size, column_count).astype(jnp.bfloat16)
    grad_value = value_total.reshape(group_size, column_count).astype(jnp.bfloat16)
    grad_qkv = jnp.concatenate([grad_query, grad_key, grad_value], 1)
    grad_wqkv = jnp.einsum("gd,gc->dc", normed_one, grad_qkv, preferred_element_type=jnp.float32)
    grad_wu = jnp.einsum("gd,gf->df", normed_two, grad_hidden, preferred_element_type=jnp.float32)
    part_one = jnp.einsum(
        "gc,dc->gd", grad_qkv, w_qkv, preferred_element_type=jnp.float32
    ).astype(jnp.bfloat16)
    part_two = jnp.einsum(
        "gf,df->gd", grad_hidden, w_hidden, preferred_element_type=jnp.float32
    ).astype(jnp.bfloat16)
    grad_in = jnp.concatenate(
        [grad_wqkv.astype(jnp.bfloat16), grad_wu.astype(jnp.bfloat16)], 1
    )
    grad_out = grad_out.astype(jnp.bfloat16)
    if ring:
        own_count = tokens.shape[0]
        parts = jnp.stack([partial_cols, part_one, part_two]).reshape(3, 4, own_count, width)
        shares, grad_in, grad_out = scatter_all(
            parts,
            grad_in.reshape(RING, width // RING, -1),
            grad_out.reshape(-1, RING, width // RING).transpose(1, 0, 2),
        )
        summed, share_one, share_two = (shares[number].astype(jnp.float32) for number in range(3))
    else:
        summed, share_one, share_two = (
            lax.psum_scatter(part, "tensor", scatter_dimension=0, tiled=True).astype(jnp.float32)
            for part in (partial_cols, part_one, part_two)
        )
        grad_in = lax.psum_scatter(grad_in, "dp", scatter_dimension=0, tiled=True)
        grad_out = lax.psum_scatter(grad_out, "dp", scatter_dimension=1, tiled=True)
    grad_in = grad_in.astype(jnp.float32)
    grad_out = grad_out.astype(jnp.float32)
    grads_in = (
        grad_in[:, :column_count],
        grad_in[:, column_count : 2 * column_count],
        grad_in[:, 2 * column_count : 3 * column_count],
        grad_in[:, 3 * column_count :],
    )
    grad_dense, grad_down = grad_out[:column_count], grad_out[column_count:]
    layer_out = (own_rows + summed + bias_dense + bias_down).astype(jnp.bfloat16)
    normed_val_one, back_one = jax.vjp(layer_norm, own_rows, gain_one, shift_one)
    normed_val_two, back_two = jax.vjp(layer_norm, own_rows, gain_two, shift_two)
    input_one, d_gain_one, d_shift_one = back_one(share_one)
    input_two, d_gain_two, d_shift_two = back_two(share_two)
    tokens_grad = out_grad.astype(jnp.float32) + input_one + input_two

    def placed(vector, full_len):
        return lax.dynamic_update_slice_in_dim(
            jnp.zeros((full_len,), jnp.float32), vector, tensor_at * vector.shape[0], 0
        )

    bias_sum = jnp.sum(out_grad, axis=0, dtype=jnp.float32)
    devices = packed_all.shape[0]
    small_terms = jnp.concatenate(
        [
            vector.reshape(devices, -1)
            for vector in (
                d_gain_one,
                d_shift_one,
                d_gain_two,
                d_shift_two,
                placed(jnp.sum(grad_query, axis=0, dtype=jnp.float32), width),
                placed(jnp.sum(grad_key, axis=0, dtype=jnp.float32), width),
                placed(jnp.sum(grad_value, axis=0, dtype=jnp.float32), width),
                bias_sum,
                placed(jnp.sum(grad_hidden, axis=0, dtype=jnp.float32), FF),
            )
        ],
        1,
    )
    if ring:
        small_terms = jnp.pad(small_terms, ((0, 0), (0, 1024 - small_terms.shape[1])))
        small_terms = small_terms.reshape(RING, 4, 8, 128).transpose(1, 0, 2, 3)
        small_total = sum_all(small_terms).reshape(-1)
    else:
        small_total = lax.psum_scatter(
            small_terms, ("dp", "tensor"), scatter_dimension=0, tiled=True
        ).reshape(-1)
    each = width // devices
    small_grads = [small_total[at * each : (at + 1) * each] for at in range(8)]
    small_grads.append(small_total[8 * each : 8 * each + FF // devices])
    return (
        layer_out,
        tokens_grad,
        small_grads[0],
        small_grads[1],
        small_grads[2],
        small_grads[3],
        grads_in[0],
        small_grads[4],
        grads_in[1],
        small_grads[5],
        grads_in[2],
        small_grads[6],
        grad_dense,
        small_grads[7],
        grads_in[3],
        small_grads[8],
        grad_down,
        small_grads[7],
    )


def solution(mesh):
    in_specs = (
        P(("dp", "tensor"), None),
        P(("dp", "tensor"), None),
        P("dp", None),
        P(("dp", "tensor")),
        P(("dp", "tensor")),
        P(("dp", "tensor")),
        P(("dp", "tensor")),
        P("dp", "tensor"),
        P(("dp", "tensor")),
        P("dp", "tensor"),
        P(("dp", "tensor")),
        P("dp", "tensor"),
        P(("dp", "tensor")),
        P("tensor", "dp"),
        P(("dp", "tensor")),
        P("dp", "tensor"),
        P(("dp", "tensor")),
        P("tensor", "dp"),
        P(("dp", "tensor")),
    )
    out_specs = (
        P(("dp", "tensor"), None),
        P(("dp", "tensor"), None),
        P(("dp", "tensor")),
        P(("dp", "tensor")),
        P(("dp", "tensor")),
        P(("dp", "tensor")),
        P("dp", "tensor"),
        P(("dp", "tensor")),
        P("dp", "tensor"),
        P(("dp", "tensor")),
        P("dp", "tensor"),
        P(("dp", "tensor")),
        P("tensor", "dp"),
        P(("dp", "tensor")),
        P("dp", "tensor"),
        P(("dp", "tensor")),
        P("tensor", "dp"),
        P(("dp", "tensor")),
    )
    ring = mesh.shape["dp"] == RING and mesh.shape["tensor"] == 4
    return jax.shard_map(
        functools.partial(per_device, ring), mesh=mesh, in_specs=in_specs, out_specs=out_specs, check_vma=False
    )
```
